32 devices in a mesh: group: 2 (over y), patch: 4 (over z), visit: 2 (over x), band: 2 (over core).
Axes of the slice: x: 2, y: 2, z: 4, core: 2. Of those that a mesh axis runs over, the one named last changes fastest.
Arguments:
- template: bfloat16 [4096, 512], P(('group', 'patch')), parts along dimension 0, may hold values from -6 to 6
- science: bfloat16 [4096, 4, 512], P(('group', 'patch'), ('visit', 'band')), parts along dimension 0, may hold values from -6 to 6
- offsets: int32 [8, 4], P(('group', 'patch'), ('visit', 'band')), parts along dimension 0, may hold values from 0 to 496
- live_flags: int32 [8, 4], P(('group', 'patch'), ('visit', 'band')), parts along dimension 0, may hold values 0 or 1
- bank: bfloat16 [16, 31], replicated, may hold values from -1 to 1
- basis_index: int32 [8, 15, 2], P(('group', 'visit', 'band')), parts along dimension 0, may hold values from 0 to 15, as said below
- coeff: float32 [8, 15], P(('group', 'visit', 'band')), parts along dimension 0, may hold values from -4 to 4
- psf_profile: bfloat16 [31], replicated, may hold values from -1 to 1
Outputs:
- difference: bfloat16 [4096, 4, 512], P(('group', 'patch'), ('visit', 'band')), parts along dimension 0
- detection: float32 [4096, 512], P(('group', 'patch', 'visit', 'band')), parts along dimension 0
The draws below stay inside these ranges and needn't reach their ends.
There are 2 independent parts, one for each index of `group`. The reference program is written for one: setup_inputs(seed, part) draws one part's arguments, and reference() takes and returns one part's arrays. A program takes and returns all parts, laid end to end along the dimension named above; an argument that names none is the same for every part. Nothing has to cross between parts.
Inputs may be any that keep to these rules, and one draw needn't show every extreme that they name: For each visit w, the 15 row profile indices basis_index[w, :, 0] are distinct, and so are the 15 column profile indices basis_index[w, :, 1].
All inputs are finite; a program needn't handle non-finite values. No bound on the sum of `live_flags` on one device may be relied on, other than what follows from the above.
Results may differ from the reference program's by a relative error of at most 0.0056.
Values may be sent and summed in bfloat16 or wider, within the bound.
A program may use at most 64 MiB of HBM per device.

```python
import jax
import jax.numpy as jnp
from jax import lax

TR = 512
TC = 512
NK = 15
KS = 31
NB = 16
VISITS = 4
ROWS = 2048
N_PATCH = 4


def draw_basis_index(key, part):
    keys = jax.random.split(jax.random.fold_in(key, 7), VISITS * 2)
    orders = jax.vmap(lambda single: jax.random.permutation(single, NB))(keys)
    picked = orders[:, :NK].reshape(VISITS, 2, NK)
    return jnp.transpose(picked, (0, 2, 1)).astype(jnp.int32)


def with_ends(array, key, least, high):
    longest = array.shape.index(max(array.shape))
    spots = []
    for shift in (0, 1):
        where = [jax.random.randint(jax.random.fold_in(key, axis), (), 0, length) for axis, length in enumerate(array.shape)]
        where[longest] = (where[longest] + shift) % array.shape[longest]
        spots.append(tuple(where))
    return array.at[spots[0]].set(least).at[spots[1]].set(high)


def shard_levels(stream_key, dims, pieces, smallest, high):
    def one(dim, parts):
        heights = jax.random.uniform(jax.random.fold_in(jax.random.fold_in(stream_key, 6), dim), (parts,), jnp.float32, smallest / len(pieces), high / len(pieces))
        return jnp.repeat(jnp.exp(heights), dims[dim] // parts).reshape((-1,) + (1,) * (len(dims) - dim - 1))

    factor_of = one(*pieces[0])
    for cut in pieces[1:]:
        factor_of = factor_of * one(*cut)
    return factor_of


def noise(own_key, extent, scale, bound, pieces=(), kind=jnp.bfloat16):
    drawn = scale * jax.random.normal(own_key, extent, jnp.float32)
    if pieces:
        drawn = drawn * shard_levels(own_key, extent, pieces, -0.22, 0.18)
    return jnp.clip(drawn, -bound, bound).astype(kind)


def setup_inputs(seed: int = 0, part: int = 0) -> dict:
    seeds = jax.random.split(jax.random.key(seed), 9)
    part_splits = jax.random.split(jax.random.fold_in(seeds[8], part), 9)
    template = noise(part_splits[0], (ROWS, TC), 1.0, 6.0, ((0, 4),))
    science = noise(part_splits[1], (ROWS, VISITS, TC), 1.0, 6.0, ((0, 4), (1, 4)))
    offsets = with_ends(jax.random.randint(part_splits[2], (N_PATCH, VISITS), 0, TR - KS // 2), jax.random.fold_in(part_splits[2], 1), 0, (TR - KS // 2) - 1).astype(jnp.int32)
    live_flags = with_ends((jax.random.randint(part_splits[3], (N_PATCH, VISITS), 0, 4) < 3).astype(jnp.int32), jax.random.fold_in(part_splits[3], 1), 0, 1)
    bank = noise(seeds[4], (NB, KS), KS ** -0.5, 1.0)
    basis_index = draw_basis_index(jax.random.fold_in(jax.random.fold_in(seeds[8], part), 71), part)
    coeff = noise(part_splits[6], (VISITS, NK), 0.26, 4.0, ((0, 4),), jnp.float32)
    psf_profile = noise(seeds[7], (KS,), KS ** -0.5, 1.0)
    return {"template": template, "science": science, "offsets": offsets, "live_flags": live_flags, "bank": bank, "basis_index": basis_index, "coeff": coeff, "psf_profile": psf_profile}


def toeplitz(profile, count):
    width = profile.shape[-1]
    lead = profile.shape[:-1]
    padded = jnp.concatenate([profile, jnp.zeros(lead + (count,), profile.dtype)], axis=-1)
    tiled = jnp.tile(padded, (1,) * len(lead) + (count,))
    tiled = tiled[..., :count * (count + width - 1)]
    return tiled.reshape(lead + (count, count + width - 1))

def profiles(bank, basis_index, coeff):
    table = bank.astype(jnp.float32)
    labels = jnp.arange(table.shape[0], dtype=jnp.int32)
    pick_row = (basis_index[:, 0:1] == labels[None, :]).astype(jnp.float32)
    pick_col = (basis_index[:, 1:2] == labels[None, :]).astype(jnp.float32)
    row_raw = jnp.dot(pick_row, table, precision=lax.Precision.HIGHEST)
    col_raw = jnp.dot(pick_col, table, precision=lax.Precision.HIGHEST)
    rowprof = (coeff[:, None] * row_raw).astype(jnp.bfloat16)
    colprof = col_raw.astype(jnp.bfloat16)
    return (rowprof, colprof)

def match_tile(window, sci, rowprof, colprof, psf):
    tile_rows, tile_cols = sci.shape
    half = psf.shape[0] // 2
    padded = jnp.pad(window, ((0, 0), (half, half)))
    colmat = toeplitz(colprof, tile_cols)
    smoothed = jnp.einsum('ri,kci->krc', padded.astype(jnp.float32), colmat.astype(jnp.float32)).astype(jnp.bfloat16)
    rowmat = toeplitz(rowprof, tile_rows)
    matched = jnp.einsum('kri,kic->rc', rowmat.astype(jnp.float32), smoothed.astype(jnp.float32))
    difference = (sci.astype(jnp.float32) - matched).astype(jnp.bfloat16)
    dpad = jnp.pad(difference, ((0, 0), (half, half)))
    pcol = toeplitz(psf, tile_cols)
    filtrow = jnp.dot(dpad, pcol.T, preferred_element_type=jnp.float32).astype(jnp.bfloat16)
    fpad = jnp.pad(filtrow, ((half, half), (0, 0)))
    prow = toeplitz(psf, tile_rows)
    filtered = jnp.dot(prow, fpad, preferred_element_type=jnp.float32)
    return (difference, filtered)

def split_rows(filtered, shift_rows, live):
    tile_rows = filtered.shape[0]
    rolled = jnp.roll(filtered, shift_rows, axis=0)
    rowid = jnp.arange(tile_rows, dtype=jnp.int32)
    mine = (rowid >= shift_rows).astype(jnp.float32) * live
    spilled = (rowid < shift_rows).astype(jnp.float32) * live
    return (rolled * mine[:, None], rolled * spilled[:, None], mine, spilled)

def reference(template, science, offsets, live_flags, bank, basis_index, coeff, psf_profile):
    half = KS // 2
    padded_tpl = jnp.concatenate([jnp.zeros((half, TC), jnp.bfloat16), template, jnp.zeros((TR + half, TC), jnp.bfloat16)], axis=0)

    def one_patch(patch_id):

        def one_visit(visit_id):
            shift_rows = offsets[patch_id, visit_id]
            start = (patch_id * TR + shift_rows).astype(jnp.int32)
            window = lax.dynamic_slice(padded_tpl, (start, jnp.int32(0)), (TR + 2 * half, TC))
            sci = lax.dynamic_slice(science, ((patch_id * TR).astype(jnp.int32), visit_id.astype(jnp.int32), jnp.int32(0)), (TR, 1, TC))[:, 0, :]
            rowprof, colprof = profiles(bank, basis_index[visit_id], coeff[visit_id])
            difference, filtered = match_tile(window, sci, rowprof, colprof, psf_profile)
            live = live_flags[patch_id, visit_id].astype(jnp.float32)
            mine, spill, mine_cover, spill_cover = split_rows(filtered, shift_rows, live)
            return (difference, mine, spill, mine_cover, spill_cover)
        diffs, mine, spill, mine_cover, spill_cover = lax.map(one_visit, jnp.arange(VISITS, dtype=jnp.int32))
        return (diffs, lax.optimization_barrier(jnp.sum(mine, axis=0)), lax.optimization_barrier(jnp.sum(spill, axis=0)), lax.optimization_barrier(jnp.sum(mine_cover, axis=0)), lax.optimization_barrier(jnp.sum(spill_cover, axis=0)))
    diffs, mine, spill, mine_cover, spill_cover = lax.map(one_patch, jnp.arange(N_PATCH, dtype=jnp.int32))
    difference = jnp.transpose(diffs, (0, 2, 1, 3)).reshape(N_PATCH * TR, VISITS, TC)
    spill_in = jnp.concatenate([jnp.zeros_like(spill[:1]), spill[:-1]], axis=0)
    cover_in = jnp.concatenate([jnp.zeros_like(spill_cover[:1]), spill_cover[:-1]], axis=0)
    accum = mine + spill_in
    cover = mine_cover + cover_in
    detection = accum * lax.rsqrt(jnp.maximum(cover, 1.0))[:, :, None]
    return (difference, detection.reshape(N_PATCH * TR, TC))
```

```python
import functools

import jax
import jax.numpy as jnp
from jax import lax
from jax.experimental import pallas as pl
from jax.experimental.pallas import tpu as pltpu
from jax.sharding import PartitionSpec as P

F32 = jnp.float32
BF16 = jnp.bfloat16
MESH = pl.DeviceIdType.MESH
GV = 16
A = 4
CB = 64


def dot(a, b):
    return jnp.dot(a, b, preferred_element_type=F32)


def dot_tn(a, b):
    return lax.dot_general(a, b, (((0,), (0,)), ((), ())), preferred_element_type=F32)


def iota(shape, axis):
    return lax.broadcasted_iota(jnp.int32, shape, axis)


def onehot(mask):
    return jnp.where(mask, 1.0, 0.0).astype(BF16)


def banded(profile, size, taps, row0, rows):
    half = taps // 2
    wide = jnp.broadcast_to(profile, (rows, size))
    rolled = pltpu.roll(wide, (row0 - half) % size, 1, stride=1, stride_axis=0)
    off = iota((rows, size), 1) - (iota((rows, size), 0) + row0)
    return jnp.where((off >= -half) & (off <= half), rolled, 0.0).astype(BF16)


def kernel(sizes, tpl, sci, off, live, bank, index, coeff, psf, diff, det,
           above, below, wts, base, tmat, rmat, eacc, ea, eb, scip, dperm, fil, land, info, pinfo,
           spill, spill_in,
           z_send, z_recv, b_send, b_recv, a_send, a_recv, i_send, i_recv,
           f_send, f_recv, s_send, s_recv):
    patches, visits, bands, taps = sizes
    peers = visits * bands
    half = taps // 2
    tr, tc = tpl.shape
    nk = index.shape[1]
    nb = bank.shape[0]
    chunk = tr // peers
    spread = tr // GV
    units = spread // A
    steps = taps - 1 + A
    g, p = lax.axis_index("group"), lax.axis_index("patch")
    v, b = lax.axis_index("visit"), lax.axis_index("band")
    me = v * bands + b

    def peer(k):
        return (g, p, k // bands, k % bands)

    barrier = pltpu.get_barrier_semaphore()
    for d in range(1, peers):
        pl.semaphore_signal(barrier, inc=1, device_id=peer((me + d) % peers), device_id_type=MESH)

    @pl.when(p > 0)
    def _():
        pl.semaphore_signal(barrier, inc=1, device_id=(g, p - 1, v, b), device_id_type=MESH)

    @pl.when(p < patches - 1)
    def _():
        pl.semaphore_signal(barrier, inc=1, device_id=(g, p + 1, v, b), device_id_type=MESH)

    pl.semaphore_wait(barrier, peers - 1 + jnp.minimum(p, 1) + jnp.minimum(patches - 1 - p, 1))

    parts = 2
    share = tr // bands
    piece = share // parts

    def z_copy(c):
        rows = pl.ds(pl.multiple_of(b * share + c * piece, 16), piece)
        return pltpu.make_async_remote_copy(
            tpl.at[rows], below.at[rows], z_send.at[c], z_recv.at[c],
            device_id=(g, p - 1, v, b), device_id_type=MESH)

    def b_copy(c):
        rows = pl.ds(pl.multiple_of(b * share + c * piece, 16), piece)
        return pltpu.make_async_remote_copy(
            below.at[rows], below.at[rows], b_send.at[c], b_recv.at[c],
            device_id=(g, p, v, 1 - b), device_id_type=MESH)

    def b_landed(c):
        rows = pl.ds(pl.multiple_of((1 - b) * share + c * piece, 16), piece)
        return pltpu.make_async_remote_copy(
            below.at[rows], below.at[rows], b_send.at[c], b_recv.at[c],
            device_id=(g, p, v, 1 - b), device_id_type=MESH)

    a_copy = pltpu.make_async_remote_copy(
        tpl.at[pl.ds(tr - 16, 16)], above, a_send, a_recv,
        device_id=(g, p + 1, v, b), device_id_type=MESH)

    @pl.when(p > 0)
    def _():
        for c in range(parts):
            z_copy(c).start()

    @pl.when(p < patches - 1)
    def _():
        a_copy.start()

    row8 = iota((8, 128), 0)
    offs = off[...]
    info[me] = jnp.where(row8 == 0, jnp.broadcast_to(offs, (8, 128)).astype(F32),
                         jnp.broadcast_to(live[...], (8, 128)).astype(F32))

    def i_copy(k, slot):
        return pltpu.make_async_remote_copy(
            info.at[slot], info.at[slot], i_send.at[k], i_recv.at[slot],
            device_id=peer(k), device_id_type=MESH)

    for d in range(1, peers):
        i_copy((me + d) % peers, me).start()

    labels = iota((nb, nk), 0)
    pick_row = onehot(labels == index[0:1, :])
    pick_col = onehot(labels == index[1:2, :])
    bk = bank[...]
    rowprof = (coeff[...] * dot_tn(bk, pick_row)).astype(BF16)
    colprof = dot_tn(pick_col, bk).astype(BF16)
    lanes = A * CB
    total = jnp.zeros((base.shape[0], lanes), F32)
    for r in range(A):
        shape = (base.shape[0], taps)
        left = dot(onehot(iota(shape, 0) == iota(shape, 1) + r), rowprof).astype(BF16)
        shape = (taps, lanes)
        right = dot(colprof, onehot(iota(shape, 1) == CB * r + taps - 1 - iota(shape, 0))).astype(BF16)
        total = total + dot(left, right)
    base[...] = total

    lane = iota((128, lanes), 1) % CB
    reach = lane - iota((128, lanes), 0) + (32 + half)
    inside = (reach >= 0) & (reach < taps)

    def weights(s, carry):
        wide = jnp.broadcast_to(base[pl.ds(s, 1), :], (128, lanes))
        rolled = pltpu.roll(wide, lanes - (32 + half), 1, stride=1, stride_axis=0)
        wts[pl.ds(pl.multiple_of(s * 128, 128), 128), :] = jnp.where(inside, rolled, 0.0).astype(BF16)
        return carry

    lax.fori_loop(0, steps, weights, 0)

    shape = (taps, tc)
    psf8 = jnp.broadcast_to(psf[...], (8, taps))
    fwd = dot(psf8, onehot(iota(shape, 1) == iota(shape, 0)))[0:1]
    rev = dot(psf8, onehot(iota(shape, 1) == taps - 1 - iota(shape, 0)))[0:1]
    for r0 in range(0, tr, 128):
        eacc[pl.ds(r0, 128), :] = banded(fwd, tc, taps, r0, 128).astype(F32)
        tmat[pl.ds(r0, 128), :] = banded(rev, tc, taps, r0, 128)
    natural = eacc[0:tr, :].astype(BF16)
    for r0 in range(0, tr, 128):
        source = iota((128, tr), 0) + r0 - offs
        source = jnp.where(source < 0, source + tr, source)
        rmat[pl.ds(r0, 128), :] = dot(onehot(iota((128, tr), 1) == source), natural).astype(BF16)

    def natural_row(f, rows, width):
        pos = iota((rows, width), 0)
        return (pos % GV) * spread + A * (pos // GV) + f

    for f in range(A):
        sel = onehot(natural_row(f, units * GV, tr) == iota((units * GV, tr), 1))
        scip[pl.ds(f * units * GV, units * GV), :] = dot(sel, sci[...]).astype(BF16)

    @pl.when(p == 0)
    def _():
        above[...] = jnp.zeros_like(above)

    @pl.when(p == patches - 1)
    def _():
        below[...] = jnp.zeros_like(below)

    @pl.when(p > 0)
    def _():
        a_copy.wait_recv()

    phase = 2 * units * GV
    for f in range(A):
        row = natural_row(f, phase, tr) + offs - half
        own = dot(onehot(row == iota((phase, tr), 1)), tpl[...])
        row = natural_row(f, phase, 16) + offs - half
        own = own + dot(onehot(row == iota((phase, 16), 1) - 16), above[...])
        eacc[pl.ds(f * phase, phase), :] = own

    @pl.when(p < patches - 1)
    def _():
        for c in range(parts):
            z_copy(c).wait_recv()
            b_copy(c).start()
        for c in range(parts):
            b_landed(c).wait_recv()

    col = iota((phase, tc), 1)
    for f in range(A):
        row = natural_row(f, phase, tr) + offs - half - tr
        got = eacc[pl.ds(f * phase, phase), :] + dot(onehot(row == iota((phase, tr), 1)), below[...])
        rows = pl.ds(f * phase, phase)
        ea[rows, :] = jnp.where(col >= 32, pltpu.roll(got, 32, 1), 0.0).astype(BF16)
        eb[rows, :] = jnp.where(col < tc - 32, pltpu.roll(got, tc - 32, 1), 0.0).astype(BF16)

    m = units * GV
    low = iota((m, 128), 1) < CB
    for blk in range(tc // 128):
        cols = slice(blk * 128, blk * 128 + 128)

        def gather(ref):
            return jnp.concatenate(
                [ref[(s % A) * phase + (s // A) * GV:(s % A) * phase + (s // A) * GV + m, cols] for s in range(steps)],
                axis=1)

        lhs = jnp.concatenate([gather(ea), gather(eb)], axis=0)
        out = dot(lhs, wts[...])
        for h in range(A // 2):
            pa = out[:m, 128 * h:128 * h + 128]
            pb = out[m:, 128 * h:128 * h + 128]
            even = jnp.where(low, pa, pltpu.roll(pb, CB, 1))
            odd = jnp.where(low, pltpu.roll(pa, CB, 1), pb)
            for f, val in ((2 * h, even), (2 * h + 1, odd)):
                rows = slice(f * m, f * m + m)
                dperm[rows, cols] = (scip[rows, cols].astype(F32) - val).astype(BF16)

    pos = iota((tr, tr), 1)
    back = (pos % GV) * spread + A * ((pos % m) // GV) + pos // m
    dnat = dot(onehot(back == iota((tr, tr), 0)), dperm[...]).astype(BF16)
    diff[...] = dnat
    filtrow = dot(dnat, tmat[...]).astype(BF16)

    def f_copy(k, slot):
        return pltpu.make_async_remote_copy(
            fil.at[k], land.at[slot], f_send.at[k], f_recv.at[slot],
            device_id=peer(k), device_id_type=MESH)

    for d in range(1, peers):
        k = (me + d) % peers
        fil[k] = dot(rmat[pl.ds(pl.multiple_of(k * chunk, 16), chunk), :], filtrow).astype(BF16)
        f_copy(k, me).start()
    land[me] = dot(rmat[pl.ds(pl.multiple_of(me * chunk, 16), chunk), :], filtrow).astype(BF16)

    for d in range(1, peers):
        i_copy((me + d) % peers, (me + d) % peers).wait_recv()

    s_copy = pltpu.make_async_remote_copy(
        spill, spill_in, s_send.at[0], s_recv.at[0], device_id=(g, p + 1, v, b), device_id_type=MESH)
    c_copy = pltpu.make_async_remote_copy(
        info, pinfo, s_send.at[1], s_recv.at[1], device_id=(g, p + 1, v, b), device_id_type=MESH)

    @pl.when(p < patches - 1)
    def _():
        c_copy.start()

    @pl.when(p == 0)
    def _():
        spill_in[...] = jnp.zeros_like(spill_in)
        pinfo[...] = jnp.zeros_like(pinfo)

    for d in range(1, peers):
        f_copy((me + d) % peers, (me + d) % peers).wait_recv()

    row = (iota((chunk, 128), 0) + me * chunk).astype(F32)
    mine, over = [], []
    for w in range(peers):
        here = row >= info[w, 0:1, :]
        lit = info[w, 1:2, :]
        mine.append(jnp.where(here, lit, 0.0))
        over.append(jnp.where(here, 0.0, lit))

    def sums(masks, cols):
        acc = masks[0] * land[0, :, cols].astype(F32)
        for w in range(1, peers):
            acc = acc + masks[w] * land[w, :, cols].astype(F32)
        return acc

    blocks = [slice(c, c + 128) for c in range(0, tc, 128)]
    for cols in blocks:
        spill[:, cols] = sums(over, cols).astype(BF16)

    @pl.when(p < patches - 1)
    def _():
        s_copy.start()

    for cols in blocks:
        det[:, cols] = sums(mine, cols)
    cover = functools.reduce(jnp.add, mine)

    @pl.when(p > 0)
    def _():
        c_copy.wait_recv()
        s_copy.wait_recv()

    for w in range(peers):
        cover = cover + jnp.where(row < pinfo[w, 0:1, :], pinfo[w, 1:2, :], 0.0)
    scale = lax.rsqrt(jnp.maximum(cover, 1.0))
    for cols in blocks:
        det[:, cols] = (det[:, cols] + spill_in[:, cols].astype(F32)) * scale

    for d in range(1, peers):
        k = (me + d) % peers
        f_copy(k, me).wait_send()
        i_copy(k, me).wait_send()

    @pl.when(p > 0)
    def _():
        for c in range(parts):
            z_copy(c).wait_send()

    @pl.when(p < patches - 1)
    def _():
        a_copy.wait_send()
        c_copy.wait_send()
        s_copy.wait_send()
        for c in range(parts):
            b_copy(c).wait_send()


def solution(mesh):
    patches, visits, bands = mesh.shape["patch"], mesh.shape["visit"], mesh.shape["band"]
    peers = visits * bands

    def on_device(template, science, offsets, live_flags, bank, basis_index, coeff, psf_profile):
        tr, tc = template.shape
        taps = bank.shape[1]
        chunk = tr // peers
        vm = pl.BlockSpec(memory_space=pltpu.VMEM)
        dma = pltpu.SemaphoreType.DMA
        steps = taps - 1 + A
        difference, detection = pl.pallas_call(
            functools.partial(kernel, (patches, visits, bands, taps)),
            out_shape=(jax.ShapeDtypeStruct((tr, tc), BF16), jax.ShapeDtypeStruct((chunk, tc), F32)),
            in_specs=[vm] * 8,
            out_specs=(vm, vm),
            scratch_shapes=[
                pltpu.VMEM((16, tc), BF16),
                pltpu.VMEM((tr, tc), BF16),
                pltpu.VMEM((steps * 128, A * CB), BF16),
                pltpu.VMEM((-(-steps // 8) * 8, A * CB), F32),
                pltpu.VMEM((tc, tc), BF16),
                pltpu.VMEM((tr, tr), BF16),
                pltpu.VMEM((2 * tr, tc), F32),
                pltpu.VMEM((2 * tr, tc), BF16),
                pltpu.VMEM((2 * tr, tc), BF16),
                pltpu.VMEM((tr, tc), BF16),
                pltpu.VMEM((tr, tc), BF16),
                pltpu.VMEM((peers, chunk, tc), BF16),
                pltpu.VMEM((peers, chunk, tc), BF16),
                pltpu.VMEM((peers, 8, 128), F32),
                pltpu.VMEM((peers, 8, 128), F32),
                pltpu.VMEM((chunk, tc), BF16),
                pltpu.VMEM((chunk, tc), BF16),
                dma((2,)), dma((2,)), dma((2,)), dma((2,)), dma, dma,
                dma((peers,)), dma((peers,)), dma((peers,)), dma((peers,)), dma((2,)), dma((2,)),
            ],
            compiler_params=pltpu.CompilerParams(
                collective_id=0, has_side_effects=True, vmem_limit_bytes=56 * 1024 * 1024),
        )(template, science[:, 0, :], offsets, live_flags, bank, basis_index[0].T, coeff, psf_profile[None, :])
        return (difference[:, None, :], detection)

    return jax.shard_map(
        on_device,
        mesh=mesh,
        in_specs=(
            P(("group", "patch"), None),
            P(("group", "patch"), ("visit", "band"), None),
            P(("group", "patch"), ("visit", "band")),
            P(("group", "patch"), ("visit", "band")),
            P(),
            P(("group", "visit", "band"), None, None),
            P(("group", "visit", "band"), None),
            P(),
        ),
        out_specs=(
            P(("group", "patch"), ("visit", "band"), None),
            P(("group", "patch", "visit", "band"), None),
        ),
        check_vma=False,
    )
```

```python
import functools

import jax
import jax.numpy as jnp
from jax import lax
from jax.experimental import pallas as pl
from jax.experimental.pallas import tpu as pltpu
from jax.sharding import PartitionSpec as P

F32 = jnp.float32
BF16 = jnp.bfloat16
MESH = pl.DeviceIdType.MESH
GV = 16
A = 4
CB = 64


def dot(a, b):
    return jnp.dot(a, b, preferred_element_type=F32)


def dot_tn(a, b):
    return lax.dot_general(a, b, (((0,), (0,)), ((), ())), preferred_element_type=F32)


def iota(shape, axis):
    return lax.broadcasted_iota(jnp.int32, shape, axis)


def onehot(mask):
    return jnp.where(mask, 1.0, 0.0).astype(BF16)


def banded(profile, size, taps, row0, rows):
    half = taps // 2
    wide = jnp.broadcast_to(profile, (rows, size))
    rolled = pltpu.roll(wide, (row0 - half) % size, 1, stride=1, stride_axis=0)
    off = iota((rows, size), 1) - (iota((rows, size), 0) + row0)
    return jnp.where((off >= -half) & (off <= half), rolled, 0.0).astype(BF16)


def kernel(sizes, tpl, sci, off, live, bank, index, coeff, psf, diff, det,
           above, below, wts, base, tmat, rmat, eacc, ea, eb, scip, dperm, fil, land, info, pinfo,
           spill, spill_in,
           z_send, z_recv, b_send, b_recv, a_send, a_recv, i_send, i_recv,
           f_send, f_recv, s_send, s_recv, c_send, c_recv):
    patches, visits, bands, taps = sizes
    peers = visits * bands
    half = taps // 2
    tr, tc = tpl.shape
    nk = index.shape[1]
    nb = bank.shape[0]
    chunk = tr // peers
    spread = tr // GV
    units = spread // A
    steps = taps - 1 + A
    g, p = lax.axis_index("group"), lax.axis_index("patch")
    v, b = lax.axis_index("visit"), lax.axis_index("band")
    me = v * bands + b

    def peer(k):
        return (g, p, k // bands, k % bands)

    barrier = pltpu.get_barrier_semaphore()
    for d in range(1, peers):
        pl.semaphore_signal(barrier, inc=1, device_id=peer((me + d) % peers), device_id_type=MESH)

    @pl.when(p > 0)
    def _():
        pl.semaphore_signal(barrier, inc=1, device_id=(g, p - 1, v, b), device_id_type=MESH)

    @pl.when(p < patches - 1)
    def _():
        pl.semaphore_signal(barrier, inc=1, device_id=(g, p + 1, v, b), device_id_type=MESH)

    pl.semaphore_wait(barrier, peers - 1 + jnp.minimum(p, 1) + jnp.minimum(patches - 1 - p, 1))

    parts = 2
    share = tr // bands
    piece = share // parts

    def z_copy(c):
        rows = pl.ds(pl.multiple_of(b * share + c * piece, 16), piece)
        return pltpu.make_async_remote_copy(
            tpl.at[rows], below.at[rows], z_send.at[c], z_recv.at[c],
            device_id=(g, p - 1, v, b), device_id_type=MESH)

    def b_copy(c):
        rows = pl.ds(pl.multiple_of(b * share + c * piece, 16), piece)
        return pltpu.make_async_remote_copy(
            below.at[rows], below.at[rows], b_send.at[c], b_recv.at[c],
            device_id=(g, p, v, 1 - b), device_id_type=MESH)

    def b_landed(c):
        rows = pl.ds(pl.multiple_of((1 - b) * share + c * piece, 16), piece)
        return pltpu.make_async_remote_copy(
            below.at[rows], below.at[rows], b_send.at[c], b_recv.at[c],
            device_id=(g, p, v, 1 - b), device_id_type=MESH)

    a_copy = pltpu.make_async_remote_copy(
        tpl.at[pl.ds(tr - 16, 16)], above, a_send, a_recv,
        device_id=(g, p + 1, v, b), device_id_type=MESH)

    @pl.when(p > 0)
    def _():
        for c in range(parts):
            z_copy(c).start()

    @pl.when(p < patches - 1)
    def _():
        a_copy.start()

    row8 = iota((8, 128), 0)
    offs = off[...]
    info[me] = jnp.where(row8 == 0, jnp.broadcast_to(offs, (8, 128)).astype(F32),
                         jnp.broadcast_to(live[...], (8, 128)).astype(F32))

    def i_copy(k, slot):
        return pltpu.make_async_remote_copy(
            info.at[slot], info.at[slot], i_send.at[k], i_recv.at[slot],
            device_id=peer(k), device_id_type=MESH)

    for d in range(1, peers):
        i_copy((me + d) % peers, me).start()

    labels = iota((nb, nk), 0)
    pick_row = onehot(labels == index[0:1, :])
    pick_col = onehot(labels == index[1:2, :])
    bk = bank[...]
    rowprof = (coeff[...] * dot_tn(bk, pick_row)).astype(BF16)
    colprof = dot_tn(pick_col, bk).astype(BF16)
    lanes = A * CB
    total = jnp.zeros((base.shape[0], lanes), F32)
    for r in range(A):
        shape = (base.shape[0], taps)
        left = dot(onehot(iota(shape, 0) == iota(shape, 1) + r), rowprof).astype(BF16)
        shape = (taps, lanes)
        right = dot(colprof, onehot(iota(shape, 1) == CB * r + taps - 1 - iota(shape, 0))).astype(BF16)
        total = total + dot(left, right)
    base[...] = total

    lane = iota((128, lanes), 1) % CB
    reach = lane - iota((128, lanes), 0) + (32 + half)
    inside = (reach >= 0) & (reach < taps)

    def weights(s, carry):
        wide = jnp.broadcast_to(base[pl.ds(s, 1), :], (128, lanes))
        rolled = pltpu.roll(wide, lanes - (32 + half), 1, stride=1, stride_axis=0)
        wts[pl.ds(pl.multiple_of(s * 128, 128), 128), :] = jnp.where(inside, rolled, 0.0).astype(BF16)
        return carry

    lax.fori_loop(0, steps, weights, 0)

    shape = (taps, tc)
    psf8 = jnp.broadcast_to(psf[...], (8, taps))
    fwd = dot(psf8, onehot(iota(shape, 1) == iota(shape, 0)))[0:1]
    rev = dot(psf8, onehot(iota(shape, 1) == taps - 1 - iota(shape, 0)))[0:1]
    for r0 in range(0, tr, 128):
        eacc[pl.ds(r0, 128), :] = banded(fwd, tc, taps, r0, 128).astype(F32)
        tmat[pl.ds(r0, 128), :] = banded(rev, tc, taps, r0, 128)
    natural = eacc[0:tr, :].astype(BF16)
    for r0 in range(0, tr, 128):
        source = iota((128, tr), 0) + r0 - offs
        source = jnp.where(source < 0, source + tr, source)
        rmat[pl.ds(r0, 128), :] = dot(onehot(iota((128, tr), 1) == source), natural).astype(BF16)

    def natural_row(f, rows, width):
        pos = iota((rows, width), 0)
        return (pos % GV) * spread + A * (pos // GV) + f

    for f in range(A):
        sel = onehot(natural_row(f, units * GV, tr) == iota((units * GV, tr), 1))
        scip[pl.ds(f * units * GV, units * GV), :] = dot(sel, sci[...]).astype(BF16)

    @pl.when(p == 0)
    def _():
        above[...] = jnp.zeros_like(above)

    @pl.when(p == patches - 1)
    def _():
        below[...] = jnp.zeros_like(below)

    @pl.when(p > 0)
    def _():
        a_copy.wait_recv()

    phase = 2 * units * GV
    for f in range(A):
        row = natural_row(f, phase, tr) + offs - half
        own = dot(onehot(row == iota((phase, tr), 1)), tpl[...])
        row = natural_row(f, phase, 16) + offs - half
        own = own + dot(onehot(row == iota((phase, 16), 1) - 16), above[...])
        eacc[pl.ds(f * phase, phase), :] = own

    @pl.when(p < patches - 1)
    def _():
        for c in range(parts):
            z_copy(c).wait_recv()
            b_copy(c).start()
        for c in range(parts):
            b_landed(c).wait_recv()

    col = iota((phase, tc), 1)
    for f in range(A):
        row = natural_row(f, phase, tr) + offs - half - tr
        got = eacc[pl.ds(f * phase, phase), :] + dot(onehot(row == iota((phase, tr), 1)), below[...])
        rows = pl.ds(f * phase, phase)
        ea[rows, :] = jnp.where(col >= 32, pltpu.roll(got, 32, 1), 0.0).astype(BF16)
        eb[rows, :] = jnp.where(col < tc - 32, pltpu.roll(got, tc - 32, 1), 0.0).astype(BF16)

    m = units * GV
    pos = iota((tr, tr), 1)
    back = (pos % GV) * spread + A * ((pos % m) // GV) + pos // m
    back = onehot(back == iota((tr, tr), 0))

    blocks = tc // 128

    def cols_of(c):
        return pl.ds(c * 128, 128)

    def chunk_of(k):
        return pl.ds(pl.multiple_of(k * chunk, 16), chunk)

    def f_copy(c, k, slot):
        return pltpu.make_async_remote_copy(
            fil.at[c, chunk_of(k)], land.at[c, slot], f_send.at[c, k], f_recv.at[c, slot],
            device_id=peer(k), device_id_type=MESH)

    others = [lax.rem(v + d, visits) for d in range(1, visits)]
    ranks = [to * bands + lax.rem(b + d, bands) for to in others for d in range(bands)]
    ranks += [v * bands + lax.rem(b + d, bands) for d in range(1, bands)]

    def filters(first, last):
        lo, hi = max(first - 1, 0) * 128, min(last + 1, blocks) * 128
        filtrow = dot(diff[:, lo:hi], tmat[lo:hi, first * 128:last * 128]).astype(BF16)
        rolled = dot(rmat[...], filtrow).astype(BF16)
        for c in range(first, last):
            fil[c] = rolled[:, (c - first) * 128:(c - first) * 128 + 128]
            for k in ranks:
                f_copy(c, k, me).start()
            land[c, me] = fil[c, chunk_of(me), :]

    m = units * GV
    low = iota((m, 128), 1) < CB
    for blk in range(tc // 128):
        cols = slice(blk * 128, blk * 128 + 128)

        def gather(ref):
            return jnp.concatenate(
                [ref[(s % A) * phase + (s // A) * GV:(s % A) * phase + (s // A) * GV + m, cols] for s in range(steps)],
                axis=1)

        lhs = jnp.concatenate([gather(ea), gather(eb)], axis=0)
        out = dot(lhs, wts[...])
        for h in range(A // 2):
            pa = out[:m, 128 * h:128 * h + 128]
            pb = out[m:, 128 * h:128 * h + 128]
            even = jnp.where(low, pa, pltpu.roll(pb, CB, 1))
            odd = jnp.where(low, pltpu.roll(pa, CB, 1), pb)
            for f, val in ((2 * h, even), (2 * h + 1, odd)):
                rows = slice(f * m, f * m + m)
                dperm[rows, cols] = (scip[rows, cols].astype(F32) - val).astype(BF16)
        if blk % 2:
            pair = slice((blk - 1) * 128, (blk + 1) * 128)
            diff[:, pair] = dot(back, dperm[:, pair]).astype(BF16)
            filters(max(blk - 2, 0), blocks if blk == blocks - 1 else blk)

    for d in range(1, peers):
        i_copy((me + d) % peers, (me + d) % peers).wait_recv()

    def s_copy(c):
        return pltpu.make_async_remote_copy(
            spill.at[c], spill_in.at[c], s_send.at[c], s_recv.at[c],
            device_id=(g, p + 1, v, b), device_id_type=MESH)

    c_copy = pltpu.make_async_remote_copy(
        info, pinfo, c_send, c_recv, device_id=(g, p + 1, v, b), device_id_type=MESH)

    @pl.when(p < patches - 1)
    def _():
        c_copy.start()

    @pl.when(p == 0)
    def _():
        spill_in[...] = jnp.zeros_like(spill_in)
        pinfo[...] = jnp.zeros_like(pinfo)

    row = (iota((chunk, 128), 0) + me * chunk).astype(F32)
    mine, over = [], []
    for w in range(peers):
        here = row >= info[w, 0:1, :]
        lit = info[w, 1:2, :]
        mine.append(jnp.where(here, lit, 0.0))
        over.append(jnp.where(here, 0.0, lit))

    def sums(masks, c):
        acc = masks[0] * land[c, 0].astype(F32)
        for w in range(1, peers):
            acc = acc + masks[w] * land[c, w].astype(F32)
        return acc

    for c in range(blocks):
        for k in ranks:
            f_copy(c, k, k).wait_recv()
        spill[c] = sums(over, c).astype(BF16)

        @pl.when(p < patches - 1)
        def _():
            s_copy(c).start()

        det[:, cols_of(c)] = sums(mine, c)
    cover = functools.reduce(jnp.add, mine)

    @pl.when(p > 0)
    def _():
        c_copy.wait_recv()

    for w in range(peers):
        cover = cover + jnp.where(row < pinfo[w, 0:1, :], pinfo[w, 1:2, :], 0.0)
    scale = lax.rsqrt(jnp.maximum(cover, 1.0))
    for c in range(blocks):
        @pl.when(p > 0)
        def _():
            s_copy(c).wait_recv()

        det[:, cols_of(c)] = (det[:, cols_of(c)] + spill_in[c].astype(F32)) * scale

    for k in ranks:
        i_copy(k, me).wait_send()
        for c in range(blocks):
            f_copy(c, k, me).wait_send()

    @pl.when(p > 0)
    def _():
        for c in range(parts):
            z_copy(c).wait_send()

    @pl.when(p < patches - 1)
    def _():
        a_copy.wait_send()
        c_copy.wait_send()
        for c in range(blocks):
            s_copy(c).wait_send()
        for c in range(parts):
            b_copy(c).wait_send()


def solution(mesh):
    patches, visits, bands = mesh.shape["patch"], mesh.shape["visit"], mesh.shape["band"]
    peers = visits * bands

    def on_device(template, science, offsets, live_flags, bank, basis_index, coeff, psf_profile):
        tr, tc = template.shape
        taps = bank.shape[1]
        chunk = tr // peers
        blocks = tc // 128
        vm = pl.BlockSpec(memory_space=pltpu.VMEM)
        dma = pltpu.SemaphoreType.DMA
        steps = taps - 1 + A
        difference, detection = pl.pallas_call(
            functools.partial(kernel, (patches, visits, bands, taps)),
            out_shape=(jax.ShapeDtypeStruct((tr, tc), BF16), jax.ShapeDtypeStruct((chunk, tc), F32)),
            in_specs=[vm] * 8,
            out_specs=(vm, vm),
            scratch_shapes=[
                pltpu.VMEM((16, tc), BF16),
                pltpu.VMEM((tr, tc), BF16),
                pltpu.VMEM((steps * 128, A * CB), BF16),
                pltpu.VMEM((-(-steps // 8) * 8, A * CB), F32),
                pltpu.VMEM((tc, tc), BF16),
                pltpu.VMEM((tr, tr), BF16),
                pltpu.VMEM((2 * tr, tc), F32),
                pltpu.VMEM((2 * tr, tc), BF16),
                pltpu.VMEM((2 * tr, tc), BF16),
                pltpu.VMEM((tr, tc), BF16),
                pltpu.VMEM((tr, tc), BF16),
                pltpu.VMEM((blocks, tr, 128), BF16),
                pltpu.VMEM((blocks, peers, chunk, 128), BF16),
                pltpu.VMEM((peers, 8, 128), F32),
                pltpu.VMEM((peers, 8, 128), F32),
                pltpu.VMEM((blocks, chunk, 128), BF16),
                pltpu.VMEM((blocks, chunk, 128), BF16),
                dma((2,)), dma((2,)), dma((2,)), dma((2,)), dma, dma,
                dma((peers,)), dma((peers,)), dma((blocks, peers)), dma((blocks, peers)),
                dma((blocks,)), dma((blocks,)), dma, dma,
            ],
            compiler_params=pltpu.CompilerParams(
                collective_id=0, has_side_effects=True, vmem_limit_bytes=56 * 1024 * 1024),
        )(template, science[:, 0, :], offsets, live_flags, bank, basis_index[0].T, coeff, psf_profile[None, :])
        return (difference[:, None, :], detection)

    return jax.shard_map(
        on_device,
        mesh=mesh,
        in_specs=(
            P(("group", "patch"), None),
            P(("group", "patch"), ("visit", "band"), None),
            P(("group", "patch"), ("visit", "band")),
            P(("group", "patch"), ("visit", "band")),
            P(),
            P(("group", "visit", "band"), None, None),
            P(("group", "visit", "band"), None),
            P(),
        ),
        out_specs=(
            P(("group", "patch"), ("visit", "band"), None),
            P(("group", "patch", "visit", "band"), None),
        ),
        check_vma=False,
    )
```
